512 devices in a mesh: wide: 128 (over z, y, core), sub: 4 (over x).
Axes of the slice: x: 4, y: 8, z: 8, core: 2. Of those that a mesh axis runs over, the one named last changes fastest.
Arguments:
- embeddings: bfloat16 [65536, 1024], P(('wide', 'sub'))
- cluster_ids: int32 [65536], P(('wide', 'sub')), may hold values from 0 to 6143, as said below
Outputs:
- nearest: float32 [65536], P(('wide', 'sub'))
The draws below stay inside these ranges and needn't reach their ends.
Inputs may be any that keep to these rules, and one draw needn't show every extreme that they name: `cluster_ids`: cluster c belongs to owner c // 48 (an index along wide). Among the 128 documents of one device, at most 2 lie in clusters of one owner; in every draw some owner has exactly 2 such documents from every device. A cluster holds at most 44 documents, and some cluster holds exactly that many.
All inputs are finite; a program needn't handle non-finite values.
Results may differ from the reference program's by a relative error of at most 0.00047.
Values may be sent and summed in bfloat16 or wider, within the bound.
No kernel may reach another device: no remote copies, remote signals or barrier semaphores. Data moves between devices by JAX's collectives and lax.ppermute only.
A program may use at most 64 MiB of HBM per device.

```python
import jax
import jax.numpy as jnp
from jax import lax

D = 1024
DOC_DEV = 128
CL_DEV = 48
CAP = 2
CLUSTER_MOST = 44
N_WIDE = 128
N_SUB = 4


def layout(key):
    key_weight, key_forced, key_raw, key_shuffle, key_tie, key_sizes = jax.random.split(key, 6)
    devices = N_WIDE * N_SUB
    total_slots = N_WIDE * CAP
    total_docs = DOC_DEV * devices
    slot_owner = jnp.arange(total_slots, dtype=jnp.int32) // CAP
    weight = jax.random.randint(key_weight, (N_WIDE,), 1, 9)
    forced = jax.random.randint(key_forced, (), 0, N_WIDE)
    raw = jax.random.randint(key_raw, (devices, total_slots), 0, 2 ** 14)
    scores = raw * weight[slot_owner][None, :] * 2048 + jnp.arange(total_slots, dtype=jnp.int32)[None, :]
    scores = scores + jnp.where(slot_owner == forced, 2 ** 29, 0)[None, :]
    scores = scores + jnp.where(jnp.arange(total_slots, dtype=jnp.int32) == total_slots - 1, 2 ** 29, 0)[None, :]
    _, chosen = lax.top_k(scores, DOC_DEV)
    chosen = jax.random.permutation(key_shuffle, chosen, axis=1, independent=True)
    doc_owner = (chosen // CAP).reshape(-1).astype(jnp.int32)
    tie_break = jax.random.permutation(key_tie, total_docs).astype(jnp.int32)
    sorted_pos = jnp.argsort(doc_owner * total_docs + tie_break).astype(jnp.int32)
    counts = jnp.zeros((N_WIDE,), jnp.int32).at[doc_owner].add(1)
    owner_start = jnp.cumsum(counts) - counts
    slot_rank = jnp.zeros((total_docs,), jnp.int32).at[sorted_pos].set(jnp.arange(total_docs, dtype=jnp.int32) - owner_start[doc_owner[sorted_pos]])
    back_rank = counts[doc_owner] - 1 - slot_rank
    sizes = jax.random.randint(key_sizes, (N_WIDE, CL_DEV), CLUSTER_MOST // 2, CLUSTER_MOST + 1)
    sizes = sizes.at[:, 0].set(CLUSTER_MOST)
    bounds = jnp.cumsum(sizes, axis=1)
    local = CL_DEV - 1 - jnp.sum((back_rank[:, None] >= bounds[doc_owner]).astype(jnp.int32), axis=1)
    return (doc_owner * CL_DEV + local).astype(jnp.int32)


def draw_cluster_ids(key, part):
    return layout(key)


def draw_embeddings(key, part):
    clusters = layout(key)
    key = jax.random.fold_in(key, 11)
    key_center, key_noise, key_spread, key_scale = jax.random.split(key, 4)
    total_docs = DOC_DEV * N_WIDE * N_SUB
    centers = jax.random.normal(key_center, (CL_DEV * N_WIDE, D), jnp.float32)
    noise = jax.random.normal(key_noise, (total_docs, D), jnp.float32)
    spread = jnp.exp(jax.random.uniform(key_spread, (total_docs, 1), jnp.float32, jnp.log(0.2), jnp.log(2.0)))
    scale = jnp.exp(jax.random.uniform(key_scale, (total_docs, 1), jnp.float32, jnp.log(0.5), jnp.log(4.0)))
    return ((centers[clusters] + spread * noise) * scale).astype(jnp.bfloat16)


def setup_inputs(seed: int = 0) -> dict:
    seeds = jax.random.split(jax.random.key(seed), 3)
    embeddings = draw_embeddings(jax.random.fold_in(seeds[2], 71), 0)
    cluster_ids = draw_cluster_ids(jax.random.fold_in(seeds[2], 71), 0)
    return {"embeddings": embeddings, "cluster_ids": cluster_ids}


def reference(embeddings, cluster_ids):
    values = embeddings.astype(jnp.float32)
    unit_rows = (values * lax.rsqrt(lax.optimization_barrier(jnp.sum(values * values, axis=1, keepdims=True)) + 1e-06)).astype(jnp.bfloat16)
    total_docs = unit_rows.shape[0]
    sorted_index = jnp.argsort(cluster_ids, stable=True).astype(jnp.int32)
    padded_rows = jnp.concatenate([jnp.zeros((CLUSTER_MOST, D), unit_rows.dtype), unit_rows[sorted_index]], axis=0)
    labels = jnp.concatenate([jnp.full((CLUSTER_MOST,), -1, jnp.int32), cluster_ids[sorted_index].astype(jnp.int32)])
    places = jnp.concatenate([jnp.full((CLUSTER_MOST,), -1, jnp.int32), sorted_index])

    def block_max(first_row):
        query_rows = lax.dynamic_slice_in_dim(padded_rows, first_row + CLUSTER_MOST, 128, 0)
        query_labels = lax.dynamic_slice_in_dim(labels, first_row + CLUSTER_MOST, 128, 0)
        query_places = lax.dynamic_slice_in_dim(places, first_row + CLUSTER_MOST, 128, 0)
        key_rows = lax.dynamic_slice_in_dim(padded_rows, first_row, CLUSTER_MOST + 128, 0)
        key_labels = lax.dynamic_slice_in_dim(labels, first_row, CLUSTER_MOST + 128, 0)
        key_places = lax.dynamic_slice_in_dim(places, first_row, CLUSTER_MOST + 128, 0)
        scores = jnp.dot(query_rows, key_rows.T, preferred_element_type=jnp.float32)
        allowed = (query_labels[:, None] == key_labels[None, :]) & (key_places[None, :] < query_places[:, None])
        return lax.optimization_barrier(jnp.max(jnp.where(allowed, scores, jnp.float32(-1.0)), axis=1))
    starts = jnp.arange(total_docs // 128, dtype=jnp.int32) * 128
    nearest_sorted = lax.map(block_max, starts).reshape(-1)
    return jnp.zeros((total_docs,), jnp.float32).at[sorted_index].set(nearest_sorted)
```

```python
import jax
import jax.numpy as jnp
from jax import lax
from jax.sharding import Mesh, PartitionSpec as P

CL_DEV = 48
EPSILON = 1e-06
META = 128
AXES = ("chip", "core", "far", "near")
PEERS = ("chip", "near")


def swap(value, axis):
    return lax.ppermute(value, axis, [(0, 1), (1, 0)])


def order_of(count, core, far):
    slot = lax.iota(jnp.int32, count)
    peer, rank = slot // 2, slot % 2
    device = (((peer // 2) * 2 + core) * 2 + far) * 2 + peer % 2
    return device * 2 + rank


def best(query, query_meta, key, key_meta):
    scores = lax.dot_general(
        query, key, (((1,), (1,)), ((), ())), preferred_element_type=jnp.float32
    )
    allowed = (query_meta[0][:, None] == key_meta[0][None, :]) & (
        key_meta[1][None, :] < query_meta[1][:, None]
    )
    return jnp.max(jnp.where(allowed, scores, jnp.float32(-1.0)), axis=1)


def per_device(embeddings, cluster_ids):
    docs, width = embeddings.shape
    peers = lax.axis_size("chip") * lax.axis_size("near")
    slots = 2 * peers
    values = embeddings.astype(jnp.float32)
    unit = (
        values * lax.rsqrt(jnp.sum(values * values, axis=1, keepdims=True) + EPSILON)
    ).astype(jnp.bfloat16)
    owner = cluster_ids // CL_DEV
    label = (cluster_ids - owner * CL_DEV + 1).astype(jnp.bfloat16)
    place = lax.iota(jnp.int32, docs)
    twin = (owner[:, None] == owner[None, :]) & (place[None, :] < place[:, None])
    slot = owner * 2 + jnp.any(twin, axis=1).astype(jnp.int32)
    pick = slot[None, :] == lax.broadcasted_iota(jnp.int32, (slots, docs), 0)
    payload = jnp.concatenate(
        [unit, jnp.broadcast_to(label[:, None], (docs, META))], axis=1
    )
    send = lax.dot_general(
        pick.astype(jnp.bfloat16),
        payload,
        (((1,), (0,)), ((), ())),
        preferred_element_type=jnp.float32,
    ).astype(jnp.bfloat16)
    recv = lax.all_to_all(
        send.reshape(peers, 2, width + META), PEERS, split_axis=0, concat_axis=0, tiled=True
    ).reshape(slots, width + META)
    rows, mark = recv[:, :width], recv[:, width]
    core, far = lax.axis_index("core"), lax.axis_index("far")
    far_rows, far_mark = swap(rows, "far"), swap(mark, "far")
    core_rows, core_mark = swap(rows, "core"), swap(mark, "core")
    both_rows, both_mark = swap(far_rows, "core"), swap(far_mark, "core")
    mine = (mark, order_of(slots, core, far))
    nearest = best(rows, mine, rows, mine)
    for key, key_mark, c, f in (
        (core_rows, core_mark, 1 - core, far),
        (far_rows, far_mark, core, 1 - far),
        (both_rows, both_mark, 1 - core, 1 - far),
    ):
        found = best(rows, mine, key, (key_mark, order_of(slots, c, f)))
        nearest = jnp.maximum(nearest, found)
    answer = lax.all_to_all(
        nearest.reshape(peers, 2), PEERS, split_axis=0, concat_axis=0, tiled=True
    ).reshape(-1)
    return jnp.sum(jnp.where(pick, answer[:, None], jnp.float32(0.0)), axis=0)


def solution(mesh):
    fine = Mesh(mesh.devices.reshape(mesh.shape["wide"] // 2, 2, 2, 2), AXES)
    return jax.shard_map(
        per_device,
        mesh=fine,
        in_specs=(P(AXES, None), P(AXES)),
        out_specs=P(AXES),
        check_vma=False,
    )
```

```python
import jax
import jax.numpy as jnp
from jax import lax
from jax.sharding import Mesh, PartitionSpec as P

CL_DEV = 48
EPSILON = 1e-06
META = 128
AXES = ("chip", "core", "far", "near")
PEERS = ("chip", "near")
EVERY = ("far", "chip", "near")


def order_of(count, core):
    slot = lax.iota(jnp.int32, count)
    rank, near, rest = slot % 2, slot // 2 % 2, slot // 4
    chips = lax.axis_size("chip")
    device = ((rest % chips * 2 + core) * 2 + rest // chips) * 2 + near
    return device * 2 + rank


def best(query, query_meta, key, key_meta):
    scores = lax.dot_general(
        query, key, (((1,), (1,)), ((), ())), preferred_element_type=jnp.float32
    )
    allowed = (query_meta[0][:, None] == key_meta[0][None, :]) & (
        key_meta[1][None, :] < query_meta[1][:, None]
    )
    return jnp.max(jnp.where(allowed, scores, jnp.float32(-1.0)), axis=1)


def per_device(embeddings, cluster_ids):
    docs, width = embeddings.shape
    owners = lax.axis_size("chip") * lax.axis_size("near")
    slots = 2 * owners
    values = embeddings.astype(jnp.float32)
    unit = (
        values * lax.rsqrt(jnp.sum(values * values, axis=1, keepdims=True) + EPSILON)
    ).astype(jnp.bfloat16)
    owner = cluster_ids // CL_DEV
    label = (cluster_ids - owner * CL_DEV + 1).astype(jnp.bfloat16)
    place = lax.iota(jnp.int32, docs)
    twin = (owner[:, None] == owner[None, :]) & (place[None, :] < place[:, None])
    slot = owner * 2 + jnp.any(twin, axis=1).astype(jnp.int32)
    pick = slot[None, :] == lax.broadcasted_iota(jnp.int32, (slots, docs), 0)
    payload = jnp.concatenate(
        [unit, jnp.broadcast_to(label[:, None], (docs, META))], axis=1
    )
    twice = jnp.concatenate([pick, pick], axis=0).astype(jnp.bfloat16)
    send = lax.dot_general(
        twice, payload, (((1,), (0,)), ((), ())), preferred_element_type=jnp.float32
    ).astype(jnp.bfloat16)
    rows = lax.all_to_all(
        send.reshape(2 * owners, 2, width + META), EVERY, split_axis=0, concat_axis=0, tiled=True
    ).reshape(2 * slots, width + META)
    other = lax.ppermute(rows, "core", [(0, 1), (1, 0)])
    core, far = lax.axis_index("core"), lax.axis_index("far")
    query = lax.dynamic_slice_in_dim(rows, far * slots, slots, 0)
    order = order_of(2 * slots, core)
    query_meta = (query[:, width], lax.dynamic_slice_in_dim(order, far * slots, slots, 0))
    here = best(query[:, :width], query_meta, rows[:, :width], (rows[:, width], order))
    there = best(
        query[:, :width],
        query_meta,
        other[:, :width],
        (other[:, width], order_of(2 * slots, 1 - core)),
    )
    nearest = jnp.maximum(here, there)
    answer = lax.all_to_all(
        nearest.reshape(owners, 2), PEERS, split_axis=0, concat_axis=0, tiled=True
    ).reshape(-1)
    return jnp.sum(jnp.where(pick, answer[:, None], jnp.float32(0.0)), axis=0)


def solution(mesh):
    fine = Mesh(mesh.devices.reshape(mesh.shape["wide"] // 2, 2, 2, 2), AXES)
    return jax.shard_map(
        per_device,
        mesh=fine,
        in_specs=(P(AXES, None), P(AXES)),
        out_specs=P(AXES),
        check_vma=False,
    )
```

```python
import jax
import jax.numpy as jnp
from jax import lax
from jax.experimental import pallas as pl
from jax.experimental.pallas import tpu as pltpu
from jax.sharding import Mesh, PartitionSpec as P

CL_DEV = 48
EPSILON = 1e-06
META = 128
AXES = ("chip", "core", "far", "near")
PEERS = ("chip", "near")


def place_kernel(ids_ref, emb_ref, out_ref, slot_ref):
    docs, width = emb_ref.shape
    slots = out_ref.shape[0]
    ids = ids_ref[...]
    owner = (ids * 43691) >> 21
    label = (ids - owner * CL_DEV + 1).astype(jnp.float32)
    slot = lax.broadcasted_iota(jnp.int32, (slots, docs), 0)
    mine = (slot >> 1) == owner
    square = (docs, docs)
    earlier = lax.broadcasted_iota(jnp.int32, square, 0) < lax.broadcasted_iota(
        jnp.int32, square, 1
    )
    seen = jnp.dot(
        mine.astype(jnp.bfloat16), earlier.astype(jnp.bfloat16), preferred_element_type=jnp.float32
    )
    pick = mine & (seen == (slot & 1).astype(jnp.float32))
    values = emb_ref[...].astype(jnp.float32)
    unit = (
        values * lax.rsqrt(jnp.sum(values * values, axis=1, keepdims=True) + EPSILON)
    ).astype(jnp.bfloat16)
    out_ref[:, :width] = jnp.dot(
        pick.astype(jnp.bfloat16), unit, preferred_element_type=jnp.float32
    ).astype(jnp.bfloat16)
    mark = jnp.sum(jnp.where(pick, label, 0.0), axis=1, keepdims=True)
    out_ref[:, width:] = jnp.broadcast_to(mark, (slots, META)).astype(jnp.bfloat16)
    slot_ref[...] = jnp.sum(jnp.where(pick, slot, 0), axis=0, keepdims=True)


def place(embeddings, cluster_ids, slots):
    docs, width = embeddings.shape
    return pl.pallas_call(
        place_kernel,
        out_shape=(
            jax.ShapeDtypeStruct((slots, width + META), jnp.bfloat16),
            jax.ShapeDtypeStruct((1, docs), jnp.int32),
        ),
        in_specs=[pl.BlockSpec(memory_space=pltpu.VMEM)] * 2,
        out_specs=(pl.BlockSpec(memory_space=pltpu.VMEM),) * 2,
        compiler_params=pltpu.CompilerParams(vmem_limit_bytes=16 * 1024 * 1024),
    )(cluster_ids.reshape(1, docs), embeddings)


def swap(value, axis):
    return lax.ppermute(value, axis, [(0, 1), (1, 0)])


def order_of(count, core, far):
    slot = lax.iota(jnp.int32, count)
    peer, rank = slot // 2, slot % 2
    device = (((peer // 2) * 2 + core) * 2 + far) * 2 + peer % 2
    return device * 2 + rank


def best(query, query_meta, key, key_meta):
    scores = lax.dot_general(
        query, key, (((1,), (1,)), ((), ())), preferred_element_type=jnp.float32
    )
    allowed = (query_meta[0][:, None] == key_meta[0][None, :]) & (
        key_meta[1][None, :] < query_meta[1][:, None]
    )
    return jnp.max(jnp.where(allowed, scores, jnp.float32(-1.0)), axis=1)


def per_device(embeddings, cluster_ids):
    docs, width = embeddings.shape
    peers = lax.axis_size("chip") * lax.axis_size("near")
    slots = 2 * peers
    send, slot = place(embeddings, cluster_ids, slots)
    recv = lax.all_to_all(
        send.reshape(peers, 2, width + META), PEERS, split_axis=0, concat_axis=0, tiled=True
    ).reshape(slots, width + META)
    rows, mark = recv[:, :width], recv[:, width]
    core, far = lax.axis_index("core"), lax.axis_index("far")
    far_rows, far_mark = swap(rows, "far"), swap(mark, "far")
    core_rows, core_mark = swap(rows, "core"), swap(mark, "core")
    both_rows, both_mark = swap(far_rows, "core"), swap(far_mark, "core")
    mine = (mark, order_of(slots, core, far))
    nearest = best(rows, mine, rows, mine)
    for key, key_mark, c, f in (
        (core_rows, core_mark, 1 - core, far),
        (far_rows, far_mark, core, 1 - far),
        (both_rows, both_mark, 1 - core, 1 - far),
    ):
        found = best(rows, mine, key, (key_mark, order_of(slots, c, f)))
        nearest = jnp.maximum(nearest, found)
    answer = lax.all_to_all(
        nearest.reshape(peers, 1, 2), PEERS, split_axis=0, concat_axis=0, tiled=True
    ).reshape(peers, 2)
    chosen = jnp.where((slot & 1) == 0, answer[:, 0:1], answer[:, 1:2])
    here = (slot >> 1) == lax.broadcasted_iota(jnp.int32, (peers, docs), 0)
    return jnp.sum(jnp.where(here, chosen, jnp.float32(0.0)), axis=0)


def solution(mesh):
    fine = Mesh(mesh.devices.reshape(mesh.shape["wide"] // 2, 2, 2, 2), AXES)
    return jax.shard_map(
        per_device,
        mesh=fine,
        in_specs=(P(AXES, None), P(AXES)),
        out_specs=P(AXES),
        check_vma=False,
    )
```

```python
import jax
import jax.numpy as jnp
from jax import lax
from jax.experimental import pallas as pl
from jax.experimental.pallas import tpu as pltpu
from jax.sharding import Mesh, PartitionSpec as P

CL_DEV = 48
EPSILON = 1e-06
META = 128
AXES = ("chip", "core", "far", "near")
PEERS = ("chip", "near")
VMEM = pl.BlockSpec(memory_space=pltpu.VMEM)
ROOM = pltpu.CompilerParams(vmem_limit_bytes=16 * 1024 * 1024)


def place_kernel(ids_ref, emb_ref, out_ref, slot_ref):
    docs, width = emb_ref.shape
    slots = out_ref.shape[0]
    ids = ids_ref[...]
    owner = (ids * 43691) >> 21
    label = (ids - owner * CL_DEV + 1).astype(jnp.float32)
    slot = lax.broadcasted_iota(jnp.int32, (slots, docs), 0)
    mine = (slot >> 1) == owner
    square = (docs, docs)
    earlier = lax.broadcasted_iota(jnp.int32, square, 0) < lax.broadcasted_iota(
        jnp.int32, square, 1
    )
    seen = jnp.dot(
        mine.astype(jnp.bfloat16), earlier.astype(jnp.bfloat16), preferred_element_type=jnp.float32
    )
    pick = mine & (seen == (slot & 1).astype(jnp.float32))
    values = emb_ref[...].astype(jnp.float32)
    unit = (
        values * lax.rsqrt(jnp.sum(values * values, axis=1, keepdims=True) + EPSILON)
    ).astype(jnp.bfloat16)
    out_ref[:, :width] = jnp.dot(
        pick.astype(jnp.bfloat16), unit, preferred_element_type=jnp.float32
    ).astype(jnp.bfloat16)
    mark = jnp.sum(jnp.where(pick, label, 0.0), axis=1, keepdims=True)
    out_ref[:, width:] = jnp.broadcast_to(mark, (slots, META)).astype(jnp.bfloat16)
    slot_ref[...] = jnp.sum(jnp.where(pick, slot, 0), axis=0, keepdims=True)


def place(embeddings, cluster_ids, slots):
    docs, width = embeddings.shape
    return pl.pallas_call(
        place_kernel,
        out_shape=(
            jax.ShapeDtypeStruct((slots, width + META), jnp.bfloat16),
            jax.ShapeDtypeStruct((1, docs), jnp.int32),
        ),
        in_specs=[VMEM, VMEM],
        out_specs=(VMEM, VMEM),
        compiler_params=ROOM,
    )(cluster_ids.reshape(1, docs), embeddings)


def take_kernel(slot_ref, answer_ref, out_ref):
    slot = slot_ref[...]
    answer = answer_ref[...]
    owners = answer.shape[0]
    chosen = jnp.where((slot & 1) == 0, answer[:, 0:1], answer[:, 1:2])
    here = (slot >> 1) == lax.broadcasted_iota(jnp.int32, (owners, slot.shape[1]), 0)
    out_ref[...] = jnp.sum(jnp.where(here, chosen, 0.0), axis=0, keepdims=True)


def take(slot, answer):
    return pl.pallas_call(
        take_kernel,
        out_shape=jax.ShapeDtypeStruct(slot.shape, jnp.float32),
        in_specs=[VMEM, VMEM],
        out_specs=VMEM,
        compiler_params=ROOM,
    )(slot, answer).reshape(-1)


def swap(value, axis):
    return lax.ppermute(value, axis, [(0, 1), (1, 0)])


def order_of(count, core, far):
    slot = lax.iota(jnp.int32, count)
    peer, rank = slot // 2, slot % 2
    device = (((peer // 2) * 2 + core) * 2 + far) * 2 + peer % 2
    return device * 2 + rank


def best(query, query_meta, key, key_meta):
    scores = lax.dot_general(
        query, key, (((1,), (1,)), ((), ())), preferred_element_type=jnp.float32
    )
    allowed = (query_meta[0][:, None] == key_meta[0][None, :]) & (
        key_meta[1][None, :] < query_meta[1][:, None]
    )
    return jnp.max(jnp.where(allowed, scores, jnp.float32(-1.0)), axis=1)


def per_device(embeddings, cluster_ids):
    docs, width = embeddings.shape
    peers = lax.axis_size("chip") * lax.axis_size("near")
    slots = 2 * peers
    send, slot = place(embeddings, cluster_ids, slots)
    recv = lax.all_to_all(
        send.reshape(peers, 2, width + META), PEERS, split_axis=0, concat_axis=0, tiled=True
    ).reshape(slots, width + META)
    core, far = lax.axis_index("core"), lax.axis_index("far")
    rows, mark = recv[:, :width], recv[:, width]
    far_rows, far_mark = swap(rows, "far"), swap(mark, "far")
    core_recv = swap(recv, "core")
    core_rows, core_mark = core_recv[:, :width], core_recv[:, width]
    mine = (mark, order_of(slots, core, far))
    twin = (core_mark, order_of(slots, 1 - core, far))
    beyond = (far_mark, order_of(slots, core, 1 - far))
    lent = swap(best(core_rows, twin, far_rows, beyond), "core")
    nearest = best(rows, mine, rows, mine)
    nearest = jnp.maximum(nearest, best(rows, mine, core_rows, twin))
    nearest = jnp.maximum(nearest, best(rows, mine, far_rows, beyond))
    nearest = jnp.maximum(nearest, lent)
    answer = lax.all_to_all(
        nearest.reshape(peers, 1, 2), PEERS, split_axis=0, concat_axis=0, tiled=True
    )
    return take(slot, answer.reshape(peers, 2))


def solution(mesh):
    fine = Mesh(mesh.devices.reshape(mesh.shape["wide"] // 2, 2, 2, 2), AXES)
    return jax.shard_map(
        per_device,
        mesh=fine,
        in_specs=(P(AXES, None), P(AXES)),
        out_specs=P(AXES),
        check_vma=False,
    )
```

```python
import jax
import jax.numpy as jnp
from jax import lax
from jax.experimental import pallas as pl
from jax.experimental.pallas import tpu as pltpu
from jax.sharding import Mesh, PartitionSpec as P

CL_DEV = 48
EPSILON = 1e-06
META = 128
AXES = ("chip", "core", "far", "near")
PEERS = ("chip", "near")
VMEM = pl.BlockSpec(memory_space=pltpu.VMEM)
ROOM = pltpu.CompilerParams(vmem_limit_bytes=16 * 1024 * 1024)


def place_kernel(ids_ref, emb_ref, out_ref, slot_ref):
    docs, width = emb_ref.shape
    slots = out_ref.shape[0]
    ids = ids_ref[...]
    owner = (ids * 43691) >> 21
    label = (ids - owner * CL_DEV + 1).astype(jnp.float32)
    slot = lax.broadcasted_iota(jnp.int32, (slots, docs), 0)
    mine = (slot >> 1) == owner
    square = (docs, docs)
    earlier = lax.broadcasted_iota(jnp.int32, square, 0) < lax.broadcasted_iota(
        jnp.int32, square, 1
    )
    seen = jnp.dot(
        mine.astype(jnp.bfloat16), earlier.astype(jnp.bfloat16), preferred_element_type=jnp.float32
    )
    pick = mine & (seen == (slot & 1).astype(jnp.float32))
    values = emb_ref[...].astype(jnp.float32)
    unit = (
        values * lax.rsqrt(jnp.sum(values * values, axis=1, keepdims=True) + EPSILON)
    ).astype(jnp.bfloat16)
    out_ref[:, :width] = jnp.dot(
        pick.astype(jnp.bfloat16), unit, preferred_element_type=jnp.float32
    ).astype(jnp.bfloat16)
    mark = jnp.sum(jnp.where(pick, label, 0.0), axis=1, keepdims=True)
    out_ref[:, width:] = jnp.broadcast_to(mark, (slots, META)).astype(jnp.bfloat16)
    slot_ref[...] = jnp.sum(jnp.where(pick, slot, 0), axis=0, keepdims=True)


def place(embeddings, cluster_ids, slots):
    docs, width = embeddings.shape
    return pl.pallas_call(
        place_kernel,
        out_shape=(
            jax.ShapeDtypeStruct((slots, width + META), jnp.bfloat16),
            jax.ShapeDtypeStruct((1, docs), jnp.int32),
        ),
        in_specs=[VMEM, VMEM],
        out_specs=(VMEM, VMEM),
        compiler_params=ROOM,
    )(cluster_ids.reshape(1, docs), embeddings)


def take_kernel(slot_ref, answer_ref, out_ref):
    slot = slot_ref[...]
    answer = answer_ref[...]
    owners = answer.shape[0]
    chosen = jnp.where((slot & 1) == 0, answer[:, 0:1], answer[:, 1:2])
    here = (slot >> 1) == lax.broadcasted_iota(jnp.int32, (owners, slot.shape[1]), 0)
    out_ref[...] = jnp.sum(jnp.where(here, chosen, 0.0), axis=0, keepdims=True)


def take(slot, answer):
    return pl.pallas_call(
        take_kernel,
        out_shape=jax.ShapeDtypeStruct(slot.shape, jnp.float32),
        in_specs=[VMEM, VMEM],
        out_specs=VMEM,
        compiler_params=ROOM,
    )(slot, answer).reshape(-1)


def found(key, key_mark, key_at, query, query_mark, query_at):
    scores = lax.dot_general(
        key, query, (((1,), (1,)), ((), ())), preferred_element_type=jnp.float32
    )

    def order(axis, at):
        slot = lax.broadcasted_iota(jnp.int32, scores.shape, axis)
        return (slot >> 2) * 16 + (slot & 3) + (at[0] * 8 + at[1] * 4)

    allowed = (key_mark == query_mark) & (order(0, key_at) < order(1, query_at))
    return jnp.max(jnp.where(allowed, scores, -1.0), axis=0, keepdims=True)


def column(ref):
    return ref[:, -META:].astype(jnp.float32)[:, 0:1]


HEAD = 16


def row_column(ref):
    row = jnp.broadcast_to(ref[...].astype(jnp.float32), (META, ref.shape[1]))
    return jnp.transpose(row)[:, 0:1]


def lent_kernel(head_ref, beyond_ref, beyond_mark_ref, twin_ref, twin_mark_ref, out_ref):
    core, far = lax.axis_index("core"), lax.axis_index("far")
    key = jnp.concatenate([head_ref[...], beyond_ref[HEAD:, :]], axis=0)
    out_ref[...] = found(
        key,
        row_column(beyond_mark_ref),
        (core, 1 - far),
        twin_ref[...],
        twin_mark_ref[...].astype(jnp.float32),
        (1 - core, far),
    )


def lend(beyond, beyond_mark, twin, twin_mark):
    slots, width = beyond.shape
    return pl.pallas_call(
        lent_kernel,
        out_shape=jax.ShapeDtypeStruct((1, slots), jnp.float32),
        in_specs=[VMEM] * 5,
        out_specs=VMEM,
        compiler_params=ROOM,
        cost_estimate=pl.CostEstimate(
            flops=2 * slots * slots * width, bytes_accessed=4 * slots * width, transcendentals=0
        ),
    )(beyond[:HEAD], beyond, beyond_mark.reshape(1, slots), twin, twin_mark.reshape(1, slots))


def mine_kernel(
    recv_ref, twin_ref, beyond_ref, mark_ref, twin_mark_ref, beyond_mark_ref, out_ref
):
    core, far = lax.axis_index("core"), lax.axis_index("far")
    query = recv_ref[:, :-META]
    mark = mark_ref[...].astype(jnp.float32)
    at = (core, far)
    best = found(query, column(recv_ref), at, query, mark, at)
    twin = found(twin_ref[...], row_column(twin_mark_ref), (1 - core, far), query, mark, at)
    beyond = found(
        beyond_ref[...], row_column(beyond_mark_ref), (core, 1 - far), query, mark, at
    )
    out_ref[...] = jnp.maximum(best, jnp.maximum(twin, beyond))


def best_of_mine(recv, twin, beyond, *marks):
    slots, width = beyond.shape
    return pl.pallas_call(
        mine_kernel,
        out_shape=jax.ShapeDtypeStruct((1, slots), jnp.float32),
        in_specs=[VMEM] * 6,
        out_specs=VMEM,
        compiler_params=ROOM,
        cost_estimate=pl.CostEstimate(
            flops=6 * slots * slots * width, bytes_accessed=6 * slots * width, transcendentals=0
        ),
    )(recv, twin, beyond, *(m.reshape(1, slots) for m in marks))


def swap(value, axis):
    return lax.ppermute(value, axis, [(0, 1), (1, 0)])


def per_device(embeddings, cluster_ids):
    docs, width = embeddings.shape
    peers = lax.axis_size("chip") * lax.axis_size("near")
    slots = 2 * peers
    send, slot = place(embeddings, cluster_ids, slots)
    recv = lax.all_to_all(
        send.reshape(peers, 2, width + META), PEERS, split_axis=0, concat_axis=0, tiled=True
    ).reshape(slots, width + META)
    rows, mark = recv[:, :width], recv[:, width]
    far_rows, far_mark = swap(rows, "far"), swap(mark, "far")
    twin, twin_mark = swap(rows, "core"), swap(mark, "core")
    lent = swap(lend(far_rows, far_mark, twin, twin_mark), "core")
    nearest = jnp.maximum(best_of_mine(recv, twin, far_rows, mark, twin_mark, far_mark), lent)
    answer = lax.all_to_all(
        nearest.reshape(peers, 1, 2), PEERS, split_axis=0, concat_axis=0, tiled=True
    )
    return take(slot, answer.reshape(peers, 2))


def solution(mesh):
    fine = Mesh(mesh.devices.reshape(mesh.shape["wide"] // 2, 2, 2, 2), AXES)
    return jax.shard_map(
        per_device,
        mesh=fine,
        in_specs=(P(AXES, None), P(AXES)),
        out_specs=P(AXES),
        check_vma=False,
    )
```

```python
import jax
import jax.numpy as jnp
from jax import lax
from jax.experimental import pallas as pl
from jax.experimental.pallas import tpu as pltpu
from jax.sharding import Mesh, PartitionSpec as P

CL_DEV = 48
EPSILON = 1e-06
META = 128
AXES = ("chip", "core", "far", "near")
PEERS = ("chip", "near")
VMEM = pl.BlockSpec(memory_space=pltpu.VMEM)
ROOM = pltpu.CompilerParams(vmem_limit_bytes=16 * 1024 * 1024)


def place_kernel(ids_ref, emb_ref, out_ref, slot_ref):
    docs, width = emb_ref.shape
    slots = out_ref.shape[0]
    ids = ids_ref[...]
    owner = (ids * 43691) >> 21
    label = (ids - owner * CL_DEV + 1).astype(jnp.float32)
    slot = lax.broadcasted_iota(jnp.int32, (slots, docs), 0)
    mine = (slot >> 1) == (owner ^ lax.axis_index("far"))
    square = (docs, docs)
    earlier = lax.broadcasted_iota(jnp.int32, square, 0) < lax.broadcasted_iota(
        jnp.int32, square, 1
    )
    seen = jnp.dot(
        mine.astype(jnp.bfloat16), earlier.astype(jnp.bfloat16), preferred_element_type=jnp.float32
    )
    pick = mine & (seen == (slot & 1).astype(jnp.float32))
    values = emb_ref[...].astype(jnp.float32)
    unit = (
        values * lax.rsqrt(jnp.sum(values * values, axis=1, keepdims=True) + EPSILON)
    ).astype(jnp.bfloat16)
    out_ref[:, :width] = jnp.dot(
        pick.astype(jnp.bfloat16), unit, preferred_element_type=jnp.float32
    ).astype(jnp.bfloat16)
    mark = jnp.sum(jnp.where(pick, label, 0.0), axis=1, keepdims=True)
    out_ref[:, width:] = jnp.broadcast_to(mark, (slots, META)).astype(jnp.bfloat16)
    slot_ref[...] = jnp.sum(jnp.where(pick, slot, 0), axis=0, keepdims=True)


def place(embeddings, cluster_ids, slots):
    docs, width = embeddings.shape
    return pl.pallas_call(
        place_kernel,
        out_shape=(
            jax.ShapeDtypeStruct((slots, width + META), jnp.bfloat16),
            jax.ShapeDtypeStruct((1, docs), jnp.int32),
        ),
        in_specs=[VMEM, VMEM],
        out_specs=(VMEM, VMEM),
        compiler_params=ROOM,
    )(cluster_ids.reshape(1, docs), embeddings)


def take_kernel(slot_ref, answer_ref, out_ref):
    slot = slot_ref[...]
    answer = answer_ref[...]
    owners = answer.shape[0]
    chosen = jnp.where((slot & 1) == 0, answer[:, 0:1], answer[:, 1:2])
    here = (slot >> 1) == lax.broadcasted_iota(jnp.int32, (owners, slot.shape[1]), 0)
    out_ref[...] = jnp.sum(jnp.where(here, chosen, 0.0), axis=0, keepdims=True)


def take(slot, answer):
    return pl.pallas_call(
        take_kernel,
        out_shape=jax.ShapeDtypeStruct(slot.shape, jnp.float32),
        in_specs=[VMEM, VMEM],
        out_specs=VMEM,
        compiler_params=ROOM,
    )(slot, answer).reshape(-1)


def found(key, key_mark, key_at, query, query_mark, query_at):
    scores = lax.dot_general(
        key, query, (((1,), (1,)), ((), ())), preferred_element_type=jnp.float32
    )

    def order(axis, at):
        slot = lax.broadcasted_iota(jnp.int32, scores.shape, axis)
        return (slot >> 2) * 16 + (slot & 3) + (at[0] * 8 + at[1] * 4)

    allowed = (key_mark == query_mark) & (order(0, key_at) < order(1, query_at))
    return jnp.max(jnp.where(allowed, scores, -1.0), axis=0, keepdims=True)


def column(ref):
    return ref[:, -META:].astype(jnp.float32)[:, 0:1]


HEAD = 16


def row_column(ref):
    row = jnp.broadcast_to(ref[...].astype(jnp.float32), (META, ref.shape[1]))
    return jnp.transpose(row)[:, 0:1]


def lent_kernel(head_ref, beyond_ref, beyond_mark_ref, twin_ref, twin_mark_ref, out_ref):
    core, far = lax.axis_index("core"), lax.axis_index("far")
    key = jnp.concatenate([head_ref[...], beyond_ref[HEAD:, :]], axis=0)
    out_ref[...] = found(
        key,
        row_column(beyond_mark_ref),
        (core, 1 - far),
        twin_ref[...],
        twin_mark_ref[...].astype(jnp.float32),
        (1 - core, far),
    )


def lend(beyond, beyond_mark, twin, twin_mark):
    slots, width = beyond.shape
    return pl.pallas_call(
        lent_kernel,
        out_shape=jax.ShapeDtypeStruct((1, slots), jnp.float32),
        in_specs=[VMEM] * 5,
        out_specs=VMEM,
        compiler_params=ROOM,
        cost_estimate=pl.CostEstimate(
            flops=2 * slots * slots * width, bytes_accessed=4 * slots * width, transcendentals=0
        ),
    )(beyond[:HEAD], beyond, beyond_mark.reshape(1, slots), twin, twin_mark.reshape(1, slots))


def mine_kernel(
    recv_ref, twin_ref, beyond_ref, mark_ref, twin_mark_ref, beyond_mark_ref, out_ref
):
    core, far = lax.axis_index("core"), lax.axis_index("far")
    query = recv_ref[:, :-META]
    mark = mark_ref[...].astype(jnp.float32)
    at = (core, far)
    best = found(query, column(recv_ref), at, query, mark, at)
    twin = found(twin_ref[...], row_column(twin_mark_ref), (1 - core, far), query, mark, at)
    beyond = found(
        beyond_ref[...], row_column(beyond_mark_ref), (core, 1 - far), query, mark, at
    )
    out_ref[...] = jnp.maximum(best, jnp.maximum(twin, beyond))


def best_of_mine(recv, twin, beyond, *marks):
    slots, width = beyond.shape
    return pl.pallas_call(
        mine_kernel,
        out_shape=jax.ShapeDtypeStruct((1, slots), jnp.float32),
        in_specs=[VMEM] * 6,
        out_specs=VMEM,
        compiler_params=ROOM,
        cost_estimate=pl.CostEstimate(
            flops=6 * slots * slots * width, bytes_accessed=6 * slots * width, transcendentals=0
        ),
    )(recv, twin, beyond, *(m.reshape(1, slots) for m in marks))


def swap(value, axis):
    return lax.ppermute(value, axis, [(0, 1), (1, 0)])


def cross(value):
    return lax.ppermute(value, ("far", "near"), [(x, 3 - x) for x in range(4)])


def per_device(embeddings, cluster_ids):
    docs, width = embeddings.shape
    peers = lax.axis_size("chip") * lax.axis_size("near")
    slots = 2 * peers
    send, slot = place(embeddings, cluster_ids, slots)
    recv = lax.all_to_all(
        send.reshape(peers, 2, width + META), PEERS, split_axis=0, concat_axis=0, tiled=True
    ).reshape(slots, width + META)
    rows, mark = recv[:, :width], recv[:, width]
    far_rows, far_mark = cross(rows), cross(mark)
    twin, twin_mark = swap(rows, "core"), swap(mark, "core")
    lent = swap(lend(far_rows, far_mark, twin, twin_mark), "core")
    nearest = jnp.maximum(best_of_mine(recv, twin, far_rows, mark, twin_mark, far_mark), lent)
    answer = lax.all_to_all(
        nearest.reshape(peers, 1, 2), PEERS, split_axis=0, concat_axis=0, tiled=True
    )
    return take(slot, answer.reshape(peers, 2))


def solution(mesh):
    fine = Mesh(mesh.devices.reshape(mesh.shape["wide"] // 2, 2, 2, 2), AXES)
    return jax.shard_map(
        per_device,
        mesh=fine,
        in_specs=(P(AXES, None), P(AXES)),
        out_specs=P(AXES),
        check_vma=False,
    )
```

```python
import jax
import jax.numpy as jnp
from jax import lax
from jax.experimental import pallas as pl
from jax.experimental.pallas import tpu as pltpu
from jax.sharding import Mesh, PartitionSpec as P

CL_DEV = 48
EPSILON = 1e-06
META = 128
AXES = ("chip", "core", "far", "near")
PEERS = ("chip", "near")
VMEM = pl.BlockSpec(memory_space=pltpu.VMEM)
ROOM = pltpu.CompilerParams(vmem_limit_bytes=16 * 1024 * 1024)


def place_kernel(ids_ref, emb_ref, out_ref, slot_ref):
    docs, width = emb_ref.shape
    peers = out_ref.shape[0]
    slots = 2 * peers
    ids = ids_ref[...]
    owner = (ids * 43691) >> 21
    label = (ids - owner * CL_DEV + 1).astype(jnp.float32)
    slot = lax.broadcasted_iota(jnp.int32, (slots, docs), 0)
    mine = (slot >> 1) == (owner ^ lax.axis_index("far"))
    square = (docs, docs)
    earlier = lax.broadcasted_iota(jnp.int32, square, 0) < lax.broadcasted_iota(
        jnp.int32, square, 1
    )
    seen = jnp.dot(
        mine.astype(jnp.bfloat16), earlier.astype(jnp.bfloat16), preferred_element_type=jnp.float32
    )
    pick = mine & (seen == (slot & 1).astype(jnp.float32))
    values = emb_ref[...].astype(jnp.float32)
    unit = (
        values * lax.rsqrt(jnp.sum(values * values, axis=1, keepdims=True) + EPSILON)
    ).astype(jnp.bfloat16)
    rows = jnp.dot(pick.astype(jnp.bfloat16), unit, preferred_element_type=jnp.float32)
    out_ref[:, :, :width] = rows.astype(jnp.bfloat16).reshape(peers, 2, width)
    mark = jnp.sum(jnp.where(pick, label, 0.0), axis=1, keepdims=True)
    marks = jnp.broadcast_to(mark, (slots, META)).astype(jnp.bfloat16)
    out_ref[:, :, width:] = marks.reshape(peers, 2, META)
    slot_ref[...] = jnp.sum(jnp.where(pick, slot, 0), axis=0, keepdims=True)


def place(embeddings, cluster_ids, slots):
    docs, width = embeddings.shape
    return pl.pallas_call(
        place_kernel,
        out_shape=(
            jax.ShapeDtypeStruct((slots // 2, 2, width + META), jnp.bfloat16),
            jax.ShapeDtypeStruct((1, docs), jnp.int32),
        ),
        in_specs=[VMEM, VMEM],
        out_specs=(VMEM, VMEM),
        compiler_params=ROOM,
    )(cluster_ids.reshape(1, docs), embeddings)


def take_kernel(slot_ref, answer_ref, out_ref):
    slot = slot_ref[...]
    answer = answer_ref[...]
    owners = answer.shape[0]
    chosen = jnp.where((slot & 1) == 0, answer[:, 0:1], answer[:, 1:2])
    here = (slot >> 1) == lax.broadcasted_iota(jnp.int32, (owners, slot.shape[1]), 0)
    out_ref[...] = jnp.sum(jnp.where(here, chosen, 0.0), axis=0, keepdims=True)


def take(slot, answer):
    return pl.pallas_call(
        take_kernel,
        out_shape=jax.ShapeDtypeStruct(slot.shape, jnp.float32),
        in_specs=[VMEM, VMEM],
        out_specs=VMEM,
        compiler_params=ROOM,
    )(slot, answer).reshape(-1)


def found(key, key_mark, key_at, query, query_mark, query_at):
    scores = lax.dot_general(
        key, query, (((1,), (1,)), ((), ())), preferred_element_type=jnp.float32
    )

    def order(axis, at):
        slot = lax.broadcasted_iota(jnp.int32, scores.shape, axis)
        return (slot >> 2) * 16 + (slot & 3) + (at[0] * 8 + at[1] * 4)

    allowed = (key_mark == query_mark) & (order(0, key_at) < order(1, query_at))
    return jnp.max(jnp.where(allowed, scores, -1.0), axis=0, keepdims=True)


def column(ref):
    return ref[:, -META:].astype(jnp.float32)[:, 0:1]


HEAD = 16


def row_column(ref):
    row = jnp.broadcast_to(ref[...].astype(jnp.float32), (META, ref.shape[1]))
    return jnp.transpose(row)[:, 0:1]


def lent_kernel(head_ref, beyond_ref, beyond_mark_ref, twin_ref, twin_mark_ref, out_ref):
    core, far = lax.axis_index("core"), lax.axis_index("far")
    key = jnp.concatenate([head_ref[...], beyond_ref[HEAD:, :]], axis=0)
    out_ref[...] = found(
        key,
        row_column(beyond_mark_ref),
        (core, 1 - far),
        twin_ref[...],
        twin_mark_ref[...].astype(jnp.float32),
        (1 - core, far),
    )


def lend(beyond, beyond_mark, twin, twin_mark):
    slots, width = beyond.shape
    return pl.pallas_call(
        lent_kernel,
        out_shape=jax.ShapeDtypeStruct((1, slots), jnp.float32),
        in_specs=[VMEM] * 5,
        out_specs=VMEM,
        compiler_params=ROOM,
        cost_estimate=pl.CostEstimate(
            flops=2 * slots * slots * width, bytes_accessed=4 * slots * width, transcendentals=0
        ),
    )(beyond[:HEAD], beyond, beyond_mark.reshape(1, slots), twin, twin_mark.reshape(1, slots))


def mine_kernel(
    recv_ref, twin_ref, beyond_ref, mark_ref, twin_mark_ref, beyond_mark_ref, out_ref
):
    core, far = lax.axis_index("core"), lax.axis_index("far")
    query = recv_ref[:, :-META]
    mark = mark_ref[...].astype(jnp.float32)
    at = (core, far)
    best = found(query, column(recv_ref), at, query, mark, at)
    twin = found(twin_ref[...], row_column(twin_mark_ref), (1 - core, far), query, mark, at)
    beyond = found(
        beyond_ref[...], row_column(beyond_mark_ref), (core, 1 - far), query, mark, at
    )
    out_ref[...] = jnp.maximum(best, jnp.maximum(twin, beyond))


def best_of_mine(recv, twin, beyond, *marks):
    slots, width = beyond.shape
    return pl.pallas_call(
        mine_kernel,
        out_shape=jax.ShapeDtypeStruct((1, slots), jnp.float32),
        in_specs=[VMEM] * 6,
        out_specs=VMEM,
        compiler_params=ROOM,
        cost_estimate=pl.CostEstimate(
            flops=6 * slots * slots * width, bytes_accessed=6 * slots * width, transcendentals=0
        ),
    )(recv, twin, beyond, *(m.reshape(1, slots) for m in marks))


def swap(value, axis):
    return lax.ppermute(value, axis, [(0, 1), (1, 0)])


def cross(value):
    return lax.ppermute(value, ("far", "near"), [(x, 3 - x) for x in range(4)])


def per_device(embeddings, cluster_ids):
    docs, width = embeddings.shape
    peers = lax.axis_size("chip") * lax.axis_size("near")
    slots = 2 * peers
    send, slot = place(embeddings, cluster_ids, slots)
    recv = lax.all_to_all(
        send, PEERS, split_axis=0, concat_axis=0, tiled=True
    ).reshape(slots, width + META)
    rows, mark = recv[:, :width], recv[:, width]
    far_rows, far_mark = cross(rows), cross(mark)
    twin, twin_mark = swap(rows, "core"), swap(mark, "core")
    lent = swap(lend(far_rows, far_mark, twin, twin_mark), "core")
    nearest = jnp.maximum(best_of_mine(recv, twin, far_rows, mark, twin_mark, far_mark), lent)
    answer = lax.all_to_all(
        nearest.reshape(peers, 1, 2), PEERS, split_axis=0, concat_axis=0, tiled=True
    )
    return take(slot, answer.reshape(peers, 2))


def solution(mesh):
    fine = Mesh(mesh.devices.reshape(mesh.shape["wide"] // 2, 2, 2, 2), AXES)
    return jax.shard_map(
        per_device,
        mesh=fine,
        in_specs=(P(AXES, None), P(AXES)),
        out_specs=P(AXES),
        check_vma=False,
    )
```

```python
import jax
import jax.numpy as jnp
from jax import lax
from jax.experimental import pallas as pl
from jax.experimental.pallas import tpu as pltpu
from jax.sharding import Mesh, PartitionSpec as P

CL_DEV = 48
EPSILON = 1e-06
META = 128
AXES = ("chip", "core", "far", "near")
PEERS = ("chip", "near")
BOTH = ("core",) + PEERS
VMEM = pl.BlockSpec(memory_space=pltpu.VMEM)
ROOM = pltpu.CompilerParams(vmem_limit_bytes=16 * 1024 * 1024)


def place_kernel(ids_ref, emb_ref, out_ref, slot_ref):
    docs, width = emb_ref.shape
    peers = out_ref.shape[0]
    slots = 2 * peers
    ids = ids_ref[...]
    owner = (ids * 43691) >> 21
    label = (ids - owner * CL_DEV + 1).astype(jnp.float32)
    slot = lax.broadcasted_iota(jnp.int32, (slots, docs), 0)
    mine = (slot >> 1) == (owner ^ lax.axis_index("far"))
    square = (docs, docs)
    earlier = lax.broadcasted_iota(jnp.int32, square, 0) < lax.broadcasted_iota(
        jnp.int32, square, 1
    )
    seen = jnp.dot(
        mine.astype(jnp.bfloat16), earlier.astype(jnp.bfloat16), preferred_element_type=jnp.float32
    )
    pick = mine & (seen == (slot & 1).astype(jnp.float32))
    values = emb_ref[...].astype(jnp.float32)
    unit = (
        values * lax.rsqrt(jnp.sum(values * values, axis=1, keepdims=True) + EPSILON)
    ).astype(jnp.bfloat16)
    rows = jnp.dot(pick.astype(jnp.bfloat16), unit, preferred_element_type=jnp.float32)
    out_ref[:, :, :width] = rows.astype(jnp.bfloat16).reshape(peers, 2, width)
    mark = jnp.sum(jnp.where(pick, label, 0.0), axis=1, keepdims=True)
    marks = jnp.broadcast_to(mark, (slots, META)).astype(jnp.bfloat16)
    out_ref[:, :, width:] = marks.reshape(peers, 2, META)
    slot_ref[...] = jnp.sum(jnp.where(pick, slot, 0), axis=0, keepdims=True)


def place(embeddings, cluster_ids, slots):
    docs, width = embeddings.shape
    return pl.pallas_call(
        place_kernel,
        out_shape=(
            jax.ShapeDtypeStruct((slots // 2, 2, width + META), jnp.bfloat16),
            jax.ShapeDtypeStruct((1, docs), jnp.int32),
        ),
        in_specs=[VMEM, VMEM],
        out_specs=(VMEM, VMEM),
        compiler_params=ROOM,
    )(cluster_ids.reshape(1, docs), embeddings)


def take_kernel(slot_ref, answer_ref, out_ref):
    slot = slot_ref[...]
    owners = answer_ref.shape[0] // 2
    answer = jnp.maximum(answer_ref[:owners, :], answer_ref[owners:, :])
    chosen = jnp.where((slot & 1) == 0, answer[:, 0:1], answer[:, 1:2])
    here = (slot >> 1) == lax.broadcasted_iota(jnp.int32, (owners, slot.shape[1]), 0)
    out_ref[...] = jnp.sum(jnp.where(here, chosen, 0.0), axis=0, keepdims=True)


def take(slot, answer):
    return pl.pallas_call(
        take_kernel,
        out_shape=jax.ShapeDtypeStruct(slot.shape, jnp.float32),
        in_specs=[VMEM, VMEM],
        out_specs=VMEM,
        compiler_params=ROOM,
    )(slot, answer).reshape(-1)


def found(key, key_mark, key_at, query, query_mark, query_at):
    scores = lax.dot_general(
        key, query, (((1,), (1,)), ((), ())), preferred_element_type=jnp.float32
    )

    def order(axis, at):
        slot = lax.broadcasted_iota(jnp.int32, scores.shape, axis)
        return (slot >> 2) * 16 + (slot & 3) + (at[0] * 8 + at[1] * 4)

    allowed = (key_mark == query_mark) & (order(0, key_at) < order(1, query_at))
    return jnp.max(jnp.where(allowed, scores, -1.0), axis=0, keepdims=True)


def column(ref):
    return ref[:, -META:].astype(jnp.float32)[:, 0:1]


HEAD = 16


def row_column(ref):
    row = jnp.broadcast_to(ref[...].astype(jnp.float32), (META, ref.shape[1]))
    return jnp.transpose(row)[:, 0:1]


def own_kernel(recv_ref, mark_ref, out_ref):
    at = (lax.axis_index("core"), lax.axis_index("far"))
    rows = recv_ref[:, :-META]
    out_ref[...] = found(rows, column(recv_ref), at, rows, mark_ref[...].astype(jnp.float32), at)


def best_own(recv, mark):
    slots = recv.shape[0]
    return pl.pallas_call(
        own_kernel,
        out_shape=jax.ShapeDtypeStruct((1, slots), jnp.float32),
        in_specs=[VMEM] * 2,
        out_specs=VMEM,
        compiler_params=ROOM,
        cost_estimate=pl.CostEstimate(
            flops=2 * slots * slots * 1024, bytes_accessed=4 * slots * 1024, transcendentals=0
        ),
    )(recv, mark.reshape(1, slots))


def score_kernel(
    recv_ref,
    own_ref,
    twin_ref,
    head_ref,
    beyond_ref,
    mark_ref,
    twin_mark_ref,
    beyond_mark_ref,
    out_ref,
):
    core, far = lax.axis_index("core"), lax.axis_index("far")
    slots = recv_ref.shape[0]
    at, twin_at, beyond_at = (core, far), (1 - core, far), (core, 1 - far)
    query, twin = recv_ref[:, :-META], twin_ref[...]
    mark = mark_ref[...].astype(jnp.float32)
    twin_mark = twin_mark_ref[...].astype(jnp.float32)
    beyond = jnp.concatenate([head_ref[...], beyond_ref[HEAD:, :]], axis=0)
    beyond_mark = row_column(beyond_mark_ref)
    mine = own_ref[...]
    mine = jnp.maximum(mine, found(twin, row_column(twin_mark_ref), twin_at, query, mark, at))
    mine = jnp.maximum(mine, found(beyond, beyond_mark, beyond_at, query, mark, at))
    lent = found(beyond, beyond_mark, beyond_at, twin, twin_mark, twin_at)
    row = lax.broadcasted_iota(jnp.int32, (2, slots), 0)
    out_ref[...] = jnp.where(row == core, mine, lent)


def best_scores(recv, own, twin, beyond, *marks):
    slots, width = beyond.shape
    return pl.pallas_call(
        score_kernel,
        out_shape=jax.ShapeDtypeStruct((2, slots), jnp.float32),
        in_specs=[VMEM] * 8,
        out_specs=VMEM,
        compiler_params=ROOM,
        cost_estimate=pl.CostEstimate(
            flops=6 * slots * slots * width, bytes_accessed=6 * slots * width, transcendentals=0
        ),
    )(recv, own, twin, beyond[:HEAD], beyond, *(m.reshape(1, slots) for m in marks))


def swap(value, axis):
    return lax.ppermute(value, axis, [(0, 1), (1, 0)])


def cross(value):
    return lax.ppermute(value, ("far", "near"), [(x, 3 - x) for x in range(4)])


def per_device(embeddings, cluster_ids):
    docs, width = embeddings.shape
    peers = lax.axis_size("chip") * lax.axis_size("near")
    slots = 2 * peers
    send, slot = place(embeddings, cluster_ids, slots)
    recv = lax.all_to_all(
        send, PEERS, split_axis=0, concat_axis=0, tiled=True
    ).reshape(slots, width + META)
    rows, mark = recv[:, :width], recv[:, width]
    far_rows, far_mark = cross(rows), cross(mark)
    twin, twin_mark = swap(rows, "core"), swap(mark, "core")
    best = best_scores(
        recv, best_own(recv, mark), twin, far_rows, mark, twin_mark, far_mark
    )
    answer = lax.all_to_all(
        best.reshape(2 * peers, 1, 2), BOTH, split_axis=0, concat_axis=0, tiled=True
    )
    return take(slot, answer.reshape(2 * peers, 2))


def solution(mesh):
    fine = Mesh(mesh.devices.reshape(mesh.shape["wide"] // 2, 2, 2, 2), AXES)
    return jax.shard_map(
        per_device,
        mesh=fine,
        in_specs=(P(AXES, None), P(AXES)),
        out_specs=P(AXES),
        check_vma=False,
    )
```

```python
import jax
import jax.numpy as jnp
from jax import lax
from jax.experimental import pallas as pl
from jax.experimental.pallas import tpu as pltpu
from jax.sharding import Mesh, PartitionSpec as P

CL_DEV = 48
EPSILON = 1e-06
META = 128
AXES = ("z2", "z1", "z0", "y2", "y1", "y0", "core", "far", "near")
PEERS = ("z0", "y0", "z1", "y1", "z2", "y2", "near")
VMEM = pl.BlockSpec(memory_space=pltpu.VMEM)
ROOM = pltpu.CompilerParams(vmem_limit_bytes=16 * 1024 * 1024)


def place_kernel(ids_ref, emb_ref, out_ref, slot_ref):
    docs, width = emb_ref.shape
    peers = out_ref.shape[0]
    slots = 2 * peers
    ids = ids_ref[...]
    owner = (ids * 43691) >> 21
    label = (ids - owner * CL_DEV + 1).astype(jnp.float32)
    slot = lax.broadcasted_iota(jnp.int32, (slots, docs), 0)
    mine = (slot >> 1) == (owner ^ lax.axis_index("far"))
    square = (docs, docs)
    earlier = lax.broadcasted_iota(jnp.int32, square, 0) < lax.broadcasted_iota(
        jnp.int32, square, 1
    )
    seen = jnp.dot(
        mine.astype(jnp.bfloat16), earlier.astype(jnp.bfloat16), preferred_element_type=jnp.float32
    )
    pick = mine & (seen == (slot & 1).astype(jnp.float32))
    values = emb_ref[...].astype(jnp.float32)
    unit = (
        values * lax.rsqrt(jnp.sum(values * values, axis=1, keepdims=True) + EPSILON)
    ).astype(jnp.bfloat16)
    rows = jnp.dot(pick.astype(jnp.bfloat16), unit, preferred_element_type=jnp.float32)
    out_ref[:, :, :width] = rows.astype(jnp.bfloat16).reshape(peers, 2, width)
    mark = jnp.sum(jnp.where(pick, label, 0.0), axis=1, keepdims=True)
    marks = jnp.broadcast_to(mark, (slots, META)).astype(jnp.bfloat16)
    out_ref[:, :, width:] = marks.reshape(peers, 2, META)
    slot_ref[...] = jnp.sum(jnp.where(pick, slot, 0), axis=0, keepdims=True)


def place(embeddings, cluster_ids, slots):
    docs, width = embeddings.shape
    return pl.pallas_call(
        place_kernel,
        out_shape=(
            jax.ShapeDtypeStruct((slots // 2, 2, width + META), jnp.bfloat16),
            jax.ShapeDtypeStruct((1, docs), jnp.int32),
        ),
        in_specs=[VMEM, VMEM],
        out_specs=(VMEM, VMEM),
        compiler_params=ROOM,
    )(cluster_ids.reshape(1, docs), embeddings)


def take_kernel(slot_ref, answer_ref, out_ref):
    slot = slot_ref[...]
    answer = answer_ref[...]
    owners = answer.shape[0]
    chosen = jnp.where((slot & 1) == 0, answer[:, 0:1], answer[:, 1:2])
    here = (slot >> 1) == lax.broadcasted_iota(jnp.int32, (owners, slot.shape[1]), 0)
    out_ref[...] = jnp.sum(jnp.where(here, chosen, 0.0), axis=0, keepdims=True)


def take(slot, answer):
    return pl.pallas_call(
        take_kernel,
        out_shape=jax.ShapeDtypeStruct(slot.shape, jnp.float32),
        in_specs=[VMEM, VMEM],
        out_specs=VMEM,
        compiler_params=ROOM,
    )(slot, answer).reshape(-1)


def found(key, key_mark, key_at, query, query_mark, query_at):
    scores = lax.dot_general(
        key, query, (((1,), (1,)), ((), ())), preferred_element_type=jnp.float32
    )

    def order(axis, at):
        shape = tuple(n if d == axis else 1 for d, n in enumerate(scores.shape))
        slot = lax.broadcasted_iota(jnp.int32, shape, axis)
        place = (slot & 1) + (at[0] * 8 + at[1] * 4)
        for bit, name in enumerate(reversed(PEERS)):
            place += ((slot >> (bit + 1)) & 1) << (len(AXES) - AXES.index(name))
        return place

    allowed = (key_mark == query_mark) & (order(0, key_at) < order(1, query_at))
    return jnp.max(jnp.where(allowed, scores, -1.0), axis=0, keepdims=True)


def column(ref):
    return ref[:, -META:].astype(jnp.float32)[:, 0:1]


HEAD = 16


def row_column(ref):
    row = jnp.broadcast_to(ref[...].astype(jnp.float32), (META, ref.shape[1]))
    return jnp.transpose(row)[:, 0:1]


def lent_kernel(head_ref, beyond_ref, beyond_mark_ref, twin_ref, twin_mark_ref, out_ref):
    core, far = lax.axis_index("core"), lax.axis_index("far")
    key = jnp.concatenate([head_ref[...], beyond_ref[HEAD:, :]], axis=0)
    out_ref[...] = found(
        key,
        row_column(beyond_mark_ref),
        (core, 1 - far),
        twin_ref[...],
        twin_mark_ref[...].astype(jnp.float32),
        (1 - core, far),
    )


def lend(beyond, beyond_mark, twin, twin_mark):
    slots, width = beyond.shape
    return pl.pallas_call(
        lent_kernel,
        out_shape=jax.ShapeDtypeStruct((1, slots), jnp.float32),
        in_specs=[VMEM] * 5,
        out_specs=VMEM,
        compiler_params=ROOM,
        cost_estimate=pl.CostEstimate(
            flops=2 * slots * slots * width, bytes_accessed=4 * slots * width, transcendentals=0
        ),
    )(beyond[:HEAD], beyond, beyond_mark.reshape(1, slots), twin, twin_mark.reshape(1, slots))


def mine_kernel(
    recv_ref, twin_ref, beyond_ref, mark_ref, twin_mark_ref, beyond_mark_ref, out_ref
):
    core, far = lax.axis_index("core"), lax.axis_index("far")
    query = recv_ref[:, :-META]
    mark = mark_ref[...].astype(jnp.float32)
    at = (core, far)
    best = found(query, column(recv_ref), at, query, mark, at)
    twin = found(twin_ref[...], row_column(twin_mark_ref), (1 - core, far), query, mark, at)
    beyond = found(
        beyond_ref[...], row_column(beyond_mark_ref), (core, 1 - far), query, mark, at
    )
    out_ref[...] = jnp.maximum(best, jnp.maximum(twin, beyond))


def best_of_mine(recv, twin, beyond, *marks):
    slots, width = beyond.shape
    return pl.pallas_call(
        mine_kernel,
        out_shape=jax.ShapeDtypeStruct((1, slots), jnp.float32),
        in_specs=[VMEM] * 6,
        out_specs=VMEM,
        compiler_params=ROOM,
        cost_estimate=pl.CostEstimate(
            flops=6 * slots * slots * width, bytes_accessed=6 * slots * width, transcendentals=0
        ),
    )(recv, twin, beyond, *(m.reshape(1, slots) for m in marks))


def swap(value, axis):
    return lax.ppermute(value, axis, [(0, 1), (1, 0)])


def cross(value):
    return lax.ppermute(value, ("far", "near"), [(x, 3 - x) for x in range(4)])


def per_device(embeddings, cluster_ids):
    docs, width = embeddings.shape
    peers = lax.axis_size(PEERS)
    slots = 2 * peers
    send, slot = place(embeddings, cluster_ids, slots)
    recv = lax.all_to_all(
        send, PEERS, split_axis=0, concat_axis=0, tiled=True
    ).reshape(slots, width + META)
    rows, mark = recv[:, :width], recv[:, width]
    far_rows, far_mark = cross(rows), cross(mark)
    twin, twin_mark = swap(rows, "core"), swap(mark, "core")
    lent = swap(lend(far_rows, far_mark, twin, twin_mark), "core")
    nearest = jnp.maximum(best_of_mine(recv, twin, far_rows, mark, twin_mark, far_mark), lent)
    answer = lax.all_to_all(
        nearest.reshape(peers, 1, 2), PEERS, split_axis=0, concat_axis=0, tiled=True
    )
    return take(slot, answer.reshape(peers, 2))


def solution(mesh):
    fine = Mesh(mesh.devices.reshape((2,) * len(AXES)), AXES)
    return jax.shard_map(
        per_device,
        mesh=fine,
        in_specs=(P(AXES, None), P(AXES)),
        out_specs=P(AXES),
        check_vma=False,
    )
```

```python
import jax
import jax.numpy as jnp
from jax import lax
from jax.experimental import pallas as pl
from jax.experimental.pallas import tpu as pltpu
from jax.sharding import Mesh, PartitionSpec as P

CL_DEV = 48
EPSILON = 1e-06
META = 128
AXES = ("z2", "z1", "z0", "y2", "y1", "y0", "core", "far", "near")
PEERS = ("y0", "z0", "y1", "z1", "y2", "z2", "near")
VMEM = pl.BlockSpec(memory_space=pltpu.VMEM)
ROOM = pltpu.CompilerParams(vmem_limit_bytes=16 * 1024 * 1024)


def place_kernel(ids_ref, emb_ref, out_ref, slot_ref):
    docs, width = emb_ref.shape
    peers = out_ref.shape[0]
    slots = 2 * peers
    ids = ids_ref[...]
    owner = (ids * 43691) >> 21
    label = (ids - owner * CL_DEV + 1).astype(jnp.float32)
    slot = lax.broadcasted_iota(jnp.int32, (slots, docs), 0)
    mine = (slot >> 1) == (owner ^ lax.axis_index("far"))
    square = (docs, docs)
    earlier = lax.broadcasted_iota(jnp.int32, square, 0) < lax.broadcasted_iota(
        jnp.int32, square, 1
    )
    seen = jnp.dot(
        mine.astype(jnp.bfloat16), earlier.astype(jnp.bfloat16), preferred_element_type=jnp.float32
    )
    pick = mine & (seen == (slot & 1).astype(jnp.float32))
    values = emb_ref[...].astype(jnp.float32)
    unit = (
        values * lax.rsqrt(jnp.sum(values * values, axis=1, keepdims=True) + EPSILON)
    ).astype(jnp.bfloat16)
    rows = jnp.dot(pick.astype(jnp.bfloat16), unit, preferred_element_type=jnp.float32)
    out_ref[:, :, :width] = rows.astype(jnp.bfloat16).reshape(peers, 2, width)
    mark = jnp.sum(jnp.where(pick, label, 0.0), axis=1, keepdims=True)
    marks = jnp.broadcast_to(mark, (slots, META)).astype(jnp.bfloat16)
    out_ref[:, :, width:] = marks.reshape(peers, 2, META)
    slot_ref[...] = jnp.sum(jnp.where(pick, slot, 0), axis=0, keepdims=True)


def place(embeddings, cluster_ids, slots):
    docs, width = embeddings.shape
    return pl.pallas_call(
        place_kernel,
        out_shape=(
            jax.ShapeDtypeStruct((slots // 2, 2, width + META), jnp.bfloat16),
            jax.ShapeDtypeStruct((1, docs), jnp.int32),
        ),
        in_specs=[VMEM, VMEM],
        out_specs=(VMEM, VMEM),
        compiler_params=ROOM,
    )(cluster_ids.reshape(1, docs), embeddings)


def take_kernel(slot_ref, answer_ref, out_ref):
    slot = slot_ref[...]
    answer = answer_ref[...]
    owners = answer.shape[0]
    chosen = jnp.where((slot & 1) == 0, answer[:, 0:1], answer[:, 1:2])
    here = (slot >> 1) == lax.broadcasted_iota(jnp.int32, (owners, slot.shape[1]), 0)
    out_ref[...] = jnp.sum(jnp.where(here, chosen, 0.0), axis=0, keepdims=True)


def take(slot, answer):
    return pl.pallas_call(
        take_kernel,
        out_shape=jax.ShapeDtypeStruct(slot.shape, jnp.float32),
        in_specs=[VMEM, VMEM],
        out_specs=VMEM,
        compiler_params=ROOM,
    )(slot, answer).reshape(-1)


def found(key, key_mark, key_at, query, query_mark, query_at):
    scores = lax.dot_general(
        key, query, (((1,), (1,)), ((), ())), preferred_element_type=jnp.float32
    )

    def order(axis, at):
        shape = tuple(n if d == axis else 1 for d, n in enumerate(scores.shape))
        slot = lax.broadcasted_iota(jnp.int32, shape, axis)
        place = (slot & 1) + (at[0] * 8 + at[1] * 4)
        for bit, name in enumerate(reversed(PEERS)):
            place += ((slot >> (bit + 1)) & 1) << (len(AXES) - AXES.index(name))
        return place

    allowed = (key_mark == query_mark) & (order(0, key_at) < order(1, query_at))
    return jnp.max(jnp.where(allowed, scores, -1.0), axis=0, keepdims=True)


def column(ref):
    return ref[:, -META:].astype(jnp.float32)[:, 0:1]


HEAD = 16


def row_column(ref):
    row = jnp.broadcast_to(ref[...].astype(jnp.float32), (META, ref.shape[1]))
    return jnp.transpose(row)[:, 0:1]


def lent_kernel(head_ref, beyond_ref, beyond_mark_ref, twin_ref, twin_mark_ref, out_ref):
    core, far = lax.axis_index("core"), lax.axis_index("far")
    key = jnp.concatenate([head_ref[...], beyond_ref[HEAD:, :]], axis=0)
    out_ref[...] = found(
        key,
        row_column(beyond_mark_ref),
        (core, 1 - far),
        twin_ref[...],
        twin_mark_ref[...].astype(jnp.float32),
        (1 - core, far),
    )


def lend(beyond, beyond_mark, twin, twin_mark):
    slots, width = beyond.shape
    return pl.pallas_call(
        lent_kernel,
        out_shape=jax.ShapeDtypeStruct((1, slots), jnp.float32),
        in_specs=[VMEM] * 5,
        out_specs=VMEM,
        compiler_params=ROOM,
        cost_estimate=pl.CostEstimate(
            flops=2 * slots * slots * width, bytes_accessed=4 * slots * width, transcendentals=0
        ),
    )(beyond[:HEAD], beyond, beyond_mark.reshape(1, slots), twin, twin_mark.reshape(1, slots))


def mine_kernel(
    recv_ref, twin_ref, beyond_ref, mark_ref, twin_mark_ref, beyond_mark_ref, out_ref
):
    core, far = lax.axis_index("core"), lax.axis_index("far")
    query = recv_ref[:, :-META]
    mark = mark_ref[...].astype(jnp.float32)
    at = (core, far)
    best = found(query, column(recv_ref), at, query, mark, at)
    twin = found(twin_ref[...], row_column(twin_mark_ref), (1 - core, far), query, mark, at)
    beyond = found(
        beyond_ref[...], row_column(beyond_mark_ref), (core, 1 - far), query, mark, at
    )
    out_ref[...] = jnp.maximum(best, jnp.maximum(twin, beyond))


def best_of_mine(recv, twin, beyond, *marks):
    slots, width = beyond.shape
    return pl.pallas_call(
        mine_kernel,
        out_shape=jax.ShapeDtypeStruct((1, slots), jnp.float32),
        in_specs=[VMEM] * 6,
        out_specs=VMEM,
        compiler_params=ROOM,
        cost_estimate=pl.CostEstimate(
            flops=6 * slots * slots * width, bytes_accessed=6 * slots * width, transcendentals=0
        ),
    )(recv, twin, beyond, *(m.reshape(1, slots) for m in marks))


def swap(value, axis):
    return lax.ppermute(value, axis, [(0, 1), (1, 0)])


def cross(value):
    return lax.ppermute(value, ("far", "near"), [(x, 3 - x) for x in range(4)])


def per_device(embeddings, cluster_ids):
    docs, width = embeddings.shape
    peers = lax.axis_size(PEERS)
    slots = 2 * peers
    send, slot = place(embeddings, cluster_ids, slots)
    recv = lax.all_to_all(
        send, PEERS, split_axis=0, concat_axis=0, tiled=True
    ).reshape(slots, width + META)
    rows, mark = recv[:, :width], recv[:, width]
    far_rows, far_mark = cross(rows), cross(mark)
    twin, twin_mark = swap(rows, "core"), swap(mark, "core")
    lent = swap(lend(far_rows, far_mark, twin, twin_mark), "core")
    nearest = jnp.maximum(best_of_mine(recv, twin, far_rows, mark, twin_mark, far_mark), lent)
    answer = lax.all_to_all(
        nearest.reshape(peers, 1, 2), PEERS, split_axis=0, concat_axis=0, tiled=True
    )
    return take(slot, answer.reshape(peers, 2))


def solution(mesh):
    fine = Mesh(mesh.devices.reshape((2,) * len(AXES)), AXES)
    return jax.shard_map(
        per_device,
        mesh=fine,
        in_specs=(P(AXES, None), P(AXES)),
        out_specs=P(AXES),
        check_vma=False,
    )
```

```python
import jax
import jax.numpy as jnp
from jax import lax
from jax.experimental import pallas as pl
from jax.experimental.pallas import tpu as pltpu
from jax.sharding import Mesh, PartitionSpec as P

CL_DEV = 48
EPSILON = 1e-06
META = 128
AXES = ("z2", "z1", "z0", "y2", "y1", "y0", "core", "far", "near")
PEERS = ("y0", "y1", "y2", "z0", "z1", "z2", "near")
VMEM = pl.BlockSpec(memory_space=pltpu.VMEM)
ROOM = pltpu.CompilerParams(vmem_limit_bytes=16 * 1024 * 1024)


def place_kernel(ids_ref, emb_ref, out_ref, slot_ref):
    docs, width = emb_ref.shape
    peers = out_ref.shape[0]
    slots = 2 * peers
    ids = ids_ref[...]
    owner = (ids * 43691) >> 21
    label = (ids - owner * CL_DEV + 1).astype(jnp.float32)
    slot = lax.broadcasted_iota(jnp.int32, (slots, docs), 0)
    mine = (slot >> 1) == (owner ^ lax.axis_index("far"))
    square = (docs, docs)
    earlier = lax.broadcasted_iota(jnp.int32, square, 0) < lax.broadcasted_iota(
        jnp.int32, square, 1
    )
    seen = jnp.dot(
        mine.astype(jnp.bfloat16), earlier.astype(jnp.bfloat16), preferred_element_type=jnp.float32
    )
    pick = mine & (seen == (slot & 1).astype(jnp.float32))
    values = emb_ref[...].astype(jnp.float32)
    unit = (
        values * lax.rsqrt(jnp.sum(values * values, axis=1, keepdims=True) + EPSILON)
    ).astype(jnp.bfloat16)
    rows = jnp.dot(pick.astype(jnp.bfloat16), unit, preferred_element_type=jnp.float32)
    out_ref[:, :, :width] = rows.astype(jnp.bfloat16).reshape(peers, 2, width)
    mark = jnp.sum(jnp.where(pick, label, 0.0), axis=1, keepdims=True)
    marks = jnp.broadcast_to(mark, (slots, META)).astype(jnp.bfloat16)
    out_ref[:, :, width:] = marks.reshape(peers, 2, META)
    slot_ref[...] = jnp.sum(jnp.where(pick, slot, 0), axis=0, keepdims=True)


def place(embeddings, cluster_ids, slots):
    docs, width = embeddings.shape
    return pl.pallas_call(
        place_kernel,
        out_shape=(
            jax.ShapeDtypeStruct((slots // 2, 2, width + META), jnp.bfloat16),
            jax.ShapeDtypeStruct((1, docs), jnp.int32),
        ),
        in_specs=[VMEM, VMEM],
        out_specs=(VMEM, VMEM),
        compiler_params=ROOM,
    )(cluster_ids.reshape(1, docs), embeddings)


def take_kernel(slot_ref, answer_ref, out_ref):
    slot = slot_ref[...]
    answer = answer_ref[...]
    owners = answer.shape[0]
    chosen = jnp.where((slot & 1) == 0, answer[:, 0:1], answer[:, 1:2])
    here = (slot >> 1) == lax.broadcasted_iota(jnp.int32, (owners, slot.shape[1]), 0)
    out_ref[...] = jnp.sum(jnp.where(here, chosen, 0.0), axis=0, keepdims=True)


def take(slot, answer):
    return pl.pallas_call(
        take_kernel,
        out_shape=jax.ShapeDtypeStruct(slot.shape, jnp.float32),
        in_specs=[VMEM, VMEM],
        out_specs=VMEM,
        compiler_params=ROOM,
    )(slot, answer).reshape(-1)


def found(key, key_mark, key_at, query, query_mark, query_at):
    scores = lax.dot_general(
        key, query, (((1,), (1,)), ((), ())), preferred_element_type=jnp.float32
    )

    def order(axis, at):
        shape = tuple(n if d == axis else 1 for d, n in enumerate(scores.shape))
        slot = lax.broadcasted_iota(jnp.int32, shape, axis)
        place = (slot & 1) + (at[0] * 8 + at[1] * 4)
        for bit, name in enumerate(reversed(PEERS)):
            place += ((slot >> (bit + 1)) & 1) << (len(AXES) - AXES.index(name))
        return place

    allowed = (key_mark == query_mark) & (order(0, key_at) < order(1, query_at))
    return jnp.max(jnp.where(allowed, scores, -1.0), axis=0, keepdims=True)


def column(ref):
    return ref[:, -META:].astype(jnp.float32)[:, 0:1]


HEAD = 16


def row_column(ref):
    row = jnp.broadcast_to(ref[...].astype(jnp.float32), (META, ref.shape[1]))
    return jnp.transpose(row)[:, 0:1]


def lent_kernel(head_ref, beyond_ref, beyond_mark_ref, twin_ref, twin_mark_ref, out_ref):
    core, far = lax.axis_index("core"), lax.axis_index("far")
    key = jnp.concatenate([head_ref[...], beyond_ref[HEAD:, :]], axis=0)
    out_ref[...] = found(
        key,
        row_column(beyond_mark_ref),
        (core, 1 - far),
        twin_ref[...],
        twin_mark_ref[...].astype(jnp.float32),
        (1 - core, far),
    )


def lend(beyond, beyond_mark, twin, twin_mark):
    slots, width = beyond.shape
    return pl.pallas_call(
        lent_kernel,
        out_shape=jax.ShapeDtypeStruct((1, slots), jnp.float32),
        in_specs=[VMEM] * 5,
        out_specs=VMEM,
        compiler_params=ROOM,
        cost_estimate=pl.CostEstimate(
            flops=2 * slots * slots * width, bytes_accessed=4 * slots * width, transcendentals=0
        ),
    )(beyond[:HEAD], beyond, beyond_mark.reshape(1, slots), twin, twin_mark.reshape(1, slots))


def mine_kernel(
    recv_ref, twin_ref, beyond_ref, mark_ref, twin_mark_ref, beyond_mark_ref, out_ref
):
    core, far = lax.axis_index("core"), lax.axis_index("far")
    query = recv_ref[:, :-META]
    mark = mark_ref[...].astype(jnp.float32)
    at = (core, far)
    best = found(query, column(recv_ref), at, query, mark, at)
    twin = found(twin_ref[...], row_column(twin_mark_ref), (1 - core, far), query, mark, at)
    beyond = found(
        beyond_ref[...], row_column(beyond_mark_ref), (core, 1 - far), query, mark, at
    )
    out_ref[...] = jnp.maximum(best, jnp.maximum(twin, beyond))


def best_of_mine(recv, twin, beyond, *marks):
    slots, width = beyond.shape
    return pl.pallas_call(
        mine_kernel,
        out_shape=jax.ShapeDtypeStruct((1, slots), jnp.float32),
        in_specs=[VMEM] * 6,
        out_specs=VMEM,
        compiler_params=ROOM,
        cost_estimate=pl.CostEstimate(
            flops=6 * slots * slots * width, bytes_accessed=6 * slots * width, transcendentals=0
        ),
    )(recv, twin, beyond, *(m.reshape(1, slots) for m in marks))


def swap(value, axis):
    return lax.ppermute(value, axis, [(0, 1), (1, 0)])


def cross(value):
    return lax.ppermute(value, ("far", "near"), [(x, 3 - x) for x in range(4)])


def per_device(embeddings, cluster_ids):
    docs, width = embeddings.shape
    peers = lax.axis_size(PEERS)
    slots = 2 * peers
    send, slot = place(embeddings, cluster_ids, slots)
    recv = lax.all_to_all(
        send, PEERS, split_axis=0, concat_axis=0, tiled=True
    ).reshape(slots, width + META)
    rows, mark = recv[:, :width], recv[:, width]
    far_rows, far_mark = cross(rows), cross(mark)
    twin, twin_mark = swap(rows, "core"), swap(mark, "core")
    lent = swap(lend(far_rows, far_mark, twin, twin_mark), "core")
    nearest = jnp.maximum(best_of_mine(recv, twin, far_rows, mark, twin_mark, far_mark), lent)
    answer = lax.all_to_all(
        nearest.reshape(peers, 1, 2), PEERS, split_axis=0, concat_axis=0, tiled=True
    )
    return take(slot, answer.reshape(peers, 2))


def solution(mesh):
    fine = Mesh(mesh.devices.reshape((2,) * len(AXES)), AXES)
    return jax.shard_map(
        per_device,
        mesh=fine,
        in_specs=(P(AXES, None), P(AXES)),
        out_specs=P(AXES),
        check_vma=False,
    )
```
